256 devices in a mesh: row: 32 (over z_hi, x, y), col: 8 (over z_lo, core).
Axes of the slice: x: 4, y: 4, z: 8 (z_hi: 2, z_lo: 4; z = z_hi * 4 + z_lo), core: 2. Of those that a mesh axis runs over, the one named last changes fastest.
Arguments:
- out_grads: bfloat16 [2048, 13824], P(None, 'col'), may hold values from -6 to 6
- inputs: bfloat16 [2048, 5120], P(None, 'row'), may hold values from -6 to 6
- out_basis: bfloat16 [13824, 13824], P('col', 'row'), may hold values from -0.0546875 to 0.0546875
- in_basis: bfloat16 [5120, 5120], P('row', 'col'), may hold values from -0.078125 to 0.078125
Outputs:
- correction: float32 [13824, 5120], P('row', 'col')
The draws below stay inside these ranges and needn't reach their ends.
All inputs are finite; a program needn't handle non-finite values.
Results may differ from the reference program's by a relative error of at most 0.0041.
Values may be sent and summed in bfloat16 or wider, within the bound.
A program may use at most 64 MiB of HBM per device.

```python
import jax
import jax.numpy as jnp

DIN = 5120
DOUT = 13824
SEQS = 2
TOK = 1024
ROWS = 2048


def shard_levels(own_key, extent, split, low, top_value):
    factor_of, own = 1.0, jax.random.fold_in(own_key, 6)
    for position, parts in split:
        heights = jnp.exp(jax.random.uniform(jax.random.fold_in(own, position), (parts,), jnp.float32, low / len(split), top_value / len(split)))
        factor_of = factor_of * jnp.repeat(heights, extent[position] // parts).reshape([-1 if axis == position else 1 for axis in range(len(extent))])
    return factor_of


def centred(stream_key, shape, spread, limit, pieces=(), kind=jnp.bfloat16):
    result = jax.random.normal(stream_key, shape, jnp.float32) * spread
    if len(pieces) > 0:
        result = shard_levels(stream_key, shape, pieces, -0.22, 0.18) * result
    return jnp.clip(result, min=-limit, max=limit).astype(kind)


def setup_inputs(seed: int = 0) -> dict:
    seeds = jax.random.split(jax.random.key(seed), 5)
    return {
        "out_grads": centred(seeds[0], (ROWS, DOUT), 1.0, 6.0, ((1, 8),)),
        "inputs": centred(seeds[1], (ROWS, DIN), 1.0, 6.0, ((1, 32),)),
        "out_basis": centred(seeds[2], (DOUT, DOUT), DOUT ** -0.5, 0.0546875, ((0, 8), (1, 32))),
        "in_basis": centred(seeds[3], (DIN, DIN), DIN ** -0.5, 0.078125, ((0, 32), (1, 8))),
    }


def reference(out_grads, inputs, out_basis, in_basis):
    out_rotated = jnp.dot(out_grads, out_basis, preferred_element_type=jnp.float32).astype(jnp.bfloat16)
    in_rotated = jnp.dot(inputs, in_basis, preferred_element_type=jnp.float32).astype(jnp.bfloat16)
    total = jnp.zeros((DOUT, DIN), jnp.float32)
    for seq_index in range(SEQS):
        out_piece = out_rotated[seq_index * TOK:(seq_index + 1) * TOK]
        in_piece = in_rotated[seq_index * TOK:(seq_index + 1) * TOK]
        rotated = jnp.dot(out_piece.T, in_piece, preferred_element_type=jnp.float32)
        total = total + rotated * rotated
    return total / jnp.float32(SEQS * TOK)
```

```python
import jax
import jax.numpy as jnp
from jax import lax
from jax.experimental import pallas as pl
from jax.experimental.pallas import tpu as pltpu
from jax.sharding import PartitionSpec as P

MESH = pl.DeviceIdType.MESH
F32 = jnp.float32
BF16 = jnp.bfloat16

ROWS = 2048
SEQ = 1024
KO = 1728
DO = 432
KI = 160
DI = 640
WP = 384
WQ = DI - WP
NC = 8
TC = SEQ // NC
NS = 2
TS = 512 // NS
TO = TS // 4
PEERS = (1, 3, 2)
RS = BF16


def kernel(
    og_hbm, inp_hbm, ob_hbm, ib_hbm, out_ref,
    og, inp, ob, obt, po, pi, ssum, sbuf, ra, rb, orot,
    xt0, xp, xq, bp, bq, fp, fq, sp, sq, rp, rq, gz, zs, zr, irp, irq,
    ld, og_sem, core_s, core_r, coreo_s, coreo_r, za_s, za_r, zb_s, zb_r, zc_s, zc_r,
    a_s, a_r, b_s, b_r, h_s, h_r, c1_s, c1_r, c2_s, c2_r,
):
    row = lax.axis_index("row")
    col = lax.axis_index("col")
    zh = row // 16
    x = (row // 4) % 4
    y = row % 4
    zl = col // 2
    core = col % 2
    pu = y * (1 - core) + x * core
    pv = x * (1 - core) + y * core

    def uv(du, dv):
        dy = du * (1 - core) + dv * core
        dx = dv * (1 - core) + du * core
        return (zh * 16 + ((x + dx) % 4) * 4 + (y + dy) % 4, col)

    other_core = (row, zl * 2 + 1 - core)
    partner = ((1 - zh) * 16 + x * 4 + y, col)

    def remote(src, dst, s, r, dev):
        return pltpu.make_async_remote_copy(
            src_ref=src, dst_ref=dst, send_sem=s, recv_sem=r, device_id=dev, device_id_type=MESH
        )

    ld_inp = pltpu.make_async_copy(inp_hbm, inp, ld.at[0])
    ld_bp = pltpu.make_async_copy(ib_hbm.at[:, 0:WP], bp.at[pl.ds(pl.multiple_of(pu * KI, 32), KI)], ld.at[1])
    ld_bq = pltpu.make_async_copy(ib_hbm.at[:, WP:DI], bq.at[pl.ds(pl.multiple_of(pv * KI, 32), KI)], ld.at[2])
    ld_ob = pltpu.make_async_copy(ob_hbm, ob, ld.at[3])
    for c in (ld_inp, ld_bp, ld_bq, ld_ob):
        c.start()
    mine = pl.multiple_of(core * SEQ, SEQ)
    theirs = pl.multiple_of((1 - core) * SEQ, SEQ)
    og_loads = []
    for jj in range(4):
        for k, base in enumerate((theirs, mine)):
            rows = pl.ds(pl.multiple_of(base + jj * 256, 256), 256)
            c = pltpu.make_async_copy(og_hbm.at[rows], og.at[rows], og_sem.at[jj, k])
            c.start()
            og_loads.append(c)

    barrier = pltpu.get_barrier_semaphore()

    def greet(dev):
        pl.semaphore_signal(barrier, inc=1, device_id=dev, device_id_type=MESH)

    for d in PEERS:
        greet(uv(d, 0))
        greet(uv(0, d))
    greet(other_core)
    greet(partner)

    @pl.when(zl > 0)
    def _():
        greet((row, col - 2))

    @pl.when(zl < 3)
    def _():
        greet((row, col + 2))

    ends = jnp.where((zl == 0) | (zl == 3), 1, 0)
    sends = []

    ld_inp.wait()
    for k in range(4):
        xt0[:, k * 512:(k + 1) * 512] = inp[k * 512:(k + 1) * 512, :].T
    xp[pl.ds(pl.multiple_of(pu * KI, 32), KI), :] = xt0[:, pl.ds(pl.multiple_of(pu * 512, 512), 512)]
    xq[pl.ds(pl.multiple_of(pv * KI, 32), KI), :] = xt0[:, pl.ds(pl.multiple_of(pv * 512, 512), 512)]
    ld_bp.wait()
    ld_bq.wait()

    pl.semaphore_wait(barrier, 10 - ends)

    a_copies = []
    for i, d in enumerate(PEERS):
        for g, (pos, dev, xb, bb) in enumerate(((pu, uv(d, 0), xp, bp), (pv, uv(0, d), xq, bq))):
            own = pl.ds(pl.multiple_of(pos * KI, 32), KI)
            to = pl.ds(pl.multiple_of(((pos + d) % 4) * 512, 512), 512)
            c = remote(bb.at[own], bb.at[own], a_s.at[0, g, i], a_r.at[0, g, i], dev)
            c.start()
            a_copies.append(c)
            c = remote(xt0.at[:, to], xb.at[own], a_s.at[1, g, i], a_r.at[1, g, i], dev)
            c.start()
            a_copies.append(c)
    sends += a_copies

    ld_ob.wait()
    obt[...] = ob[...].T

    def out_product(base, jj, k):
        og_loads[jj * 2 + k].wait()
        g = og[pl.ds(pl.multiple_of(base + jj * 256, 256), 256), :]
        return lax.dot_general(obt[...], g, (((1,), (1,)), ((), ())), preferred_element_type=F32)

    core_copies = []

    def out_theirs(jj):
        po[jj] = out_product(theirs, jj, 0)
        c = remote(po.at[jj], pi.at[jj], core_s.at[jj], core_r.at[jj], other_core)
        c.start()
        core_copies.append(c)
        sends.append(c)

    def role(j):
        return zl if j % 2 == 0 else 3 - zl

    def step(j, by):
        return (row, col + 2 * by if j % 2 == 0 else col - 2 * by)

    def za(j, by):
        return remote(sbuf.at[j], ra.at[j], za_s.at[j], za_r.at[j], step(j, by))

    def zb(j):
        return remote(sbuf.at[j], rb.at[j], zb_s.at[j], zb_r.at[j], step(j, -1))

    def tokens(j):
        return pl.ds(pl.multiple_of(mine + j * TC, TC), TC)

    def zc(j, by, k):
        at = orot.at[:, tokens(j)]
        return remote(at, at, zc_s.at[j, k], zc_r.at[j], step(j, by))

    def co(j):
        at = orot.at[:, tokens(j)]
        return remote(at, at, coreo_s.at[j], coreo_r.at[j], other_core)

    def out_mine(jj):
        own = out_product(mine, jj, 1)
        core_copies[jj].wait_recv()
        total = own + pi[jj]
        for h in range(2):
            j = 2 * jj + h
            part = total[:, h * TC:(h + 1) * TC]
            ssum[j] = part
            p = role(j)

            @pl.when(p == 0)
            def _():
                sbuf[j] = part.astype(BF16)
                za(j, 1).start()

            @pl.when(p == 3)
            def _():
                sbuf[j] = part.astype(BF16)
                za(j, -1).start()

    def out_a(j):
        @pl.when(role(j) == 2)
        def _():
            za(j, 1).wait_recv()
            sbuf[j] = (ssum[j] + ra[j].astype(F32)).astype(BF16)
            zb(j).start()

    def out_b(j):
        @pl.when(role(j) == 1)
        def _():
            za(j, 1).wait_recv()
            zb(j).wait_recv()
            orot[:, tokens(j)] = (ssum[j] + ra[j].astype(F32) + rb[j].astype(F32)).astype(BF16)
            zc(j, -1, 0).start()
            zc(j, 1, 1).start()
            co(j).start()

    def out_c(j):
        @pl.when(role(j) == 2)
        def _():
            zc(j, 1, 0).wait_recv()
            zc(j, 1, 0).start()
            co(j).start()

    def out_d(j):
        p = role(j)

        @pl.when((p == 0) | (p == 3))
        def _():
            zc(j, 1, 0).wait_recv()
            co(j).start()

    def out_end(j):
        co(j).wait_recv()
        co(j).wait_send()
        p = role(j)

        @pl.when(p == 0)
        def _():
            za(j, 1).wait_send()

        @pl.when(p == 3)
        def _():
            za(j, -1).wait_send()

        @pl.when(p == 2)
        def _():
            zb(j).wait_send()
            zc(j, 1, 0).wait_send()

        @pl.when(p == 1)
        def _():
            zc(j, -1, 0).wait_send()
            zc(j, 1, 1).wait_send()

    blocks = ((0, pv, lambda d: uv(0, d), xp, bp, fp, sp, rp), (1, pu, lambda d: uv(d, 0), xq, bq, fq, sq, rq))
    b_copies = {}

    def in_partial(st):
        for g, pos, dev, xb, bb, f, s, r in blocks:
            part = jnp.dot(xb[:, st * TS:(st + 1) * TS].T, bb[...], preferred_element_type=F32)
            f[st] = part
            s[st] = part.astype(RS)
            for i, d in enumerate(PEERS):
                to = pl.ds(pl.multiple_of(((pos + d) % 4) * TO, TO), TO)
                c = remote(s.at[st, to], r.at[st, i], b_s.at[st, g, i], b_r.at[st, g, i], dev(d))
                c.start()
                b_copies[st, g, i] = c
                sends.append(c)

    h_copies = {}

    def in_cross(st):
        for g, pos, dev, xb, bb, f, s, r in blocks:
            for i in range(3):
                b_copies[st, g, i].wait_recv()
            total = f[st, pl.ds(pl.multiple_of(pos * TO, TO), TO), :]
            for i in range(3):
                total = total + r[st, i].astype(F32)
            lanes = slice(0, WP) if g == 0 else slice(WP, DI)
            gz[st, :, lanes] = total
            zs[st, :, lanes] = total.astype(BF16)
        c = remote(zs.at[st], zr.at[st], h_s.at[st], h_r.at[st], partner)
        c.start()
        h_copies[st] = c
        sends.append(c)

    gather = (
        (0, irp, pu, pv, lambda d: uv(d, 0), lambda d: uv(0, d)),
        (1, irq, pv, pu, lambda d: uv(0, d), lambda d: uv(d, 0)),
    )
    c2 = {}

    def sub(buf, first, second, st):
        return buf.at[pl.ds(pl.multiple_of(first * 512 + st * TS + second * TO, TO), TO)]

    def c2_send(st, g, k, side):
        _, buf, first, second, along, across = gather[g]
        at = sub(buf, first, (second + k) % 4, st)
        c = remote(at, at, c2_s.at[st, g, side, k], c2_r.at[st, g, side, k], along(1 if side == 0 else 3))
        c.start()
        c2[st, g, side, k] = c
        sends.append(c)

    c1 = {}

    def in_round(st):
        h_copies[st].wait_recv()
        for g, buf, first, second, along, across in gather:
            lanes = slice(0, WP) if g == 0 else slice(WP, DI)
            whole = gz[st, :, lanes] + zr[st, :, lanes].astype(F32)
            sub(buf, first, second, st)[...] = whole.astype(BF16)
        for g, buf, first, second, along, across in gather:
            at = sub(buf, first, second, st)
            for i, d in enumerate(PEERS):
                c = remote(at, at, c1_s.at[st, g, i], c1_r.at[st, g, i], across(d))
                c.start()
                c1[st, g, i] = c
                sends.append(c)
        for g in range(2):
            for side in range(2):
                c2_send(st, g, 0, side)

    def in_spread(st, i):
        k = (4 - PEERS[i]) % 4
        for g in range(2):
            c1[st, g, i].wait_recv()
            for side in range(2):
                c2_send(st, g, k, side)

    ORDER = (0, 3, 1, 2)
    c3 = {}

    def in_forward(st, side):
        for k in ORDER[:2] if side == 0 else ORDER[2:]:
            for g, buf, first, second, along, across in gather:
                c2[st, g, side, k].wait_recv()
                at = sub(buf, (first + (3 if side == 0 else 1)) % 4, (second + k) % 4, st)
                c = remote(at, at, c2_s.at[st, g, 2, k], c2_r.at[st, g, 2, k], along(1 if side == 0 else 3))
                c.start()
                c3[st, g, k] = c
                sends.append(c)

    def in_end(st):
        for g in range(2):
            for k in ORDER[2:]:
                c2[st, g, 0, k].wait_recv()
            for k in ORDER[:2]:
                c2[st, g, 1, k].wait_recv()
            for k in range(4):
                c3[st, g, k].wait_recv()

    for jj in range(4):
        out_theirs(jj)
        out_mine(jj)
    out_a(0)
    out_a(1)
    for c in a_copies:
        c.wait_recv()
    in_partial(0)
    in_partial(1)
    out_b(0)
    out_a(2)
    out_b(1)
    out_a(3)
    in_cross(0)
    out_c(0)
    out_b(2)
    out_a(4)
    in_cross(1)
    out_c(1)
    out_d(0)
    out_b(3)
    out_a(5)
    in_round(0)
    out_c(2)
    out_d(1)
    out_b(4)
    out_a(6)
    in_round(1)
    for i in range(3):
        in_spread(0, i)
    out_c(3)
    out_d(2)
    out_b(5)
    out_a(7)
    for i in range(3):
        in_spread(1, i)
    out_c(4)
    out_d(3)
    out_b(6)
    in_forward(0, 0)
    in_forward(0, 1)
    out_c(5)
    out_d(4)
    out_b(7)
    in_forward(1, 0)
    in_forward(1, 1)
    out_c(6)
    out_d(5)
    out_c(7)
    out_d(6)
    out_d(7)
    for j in range(NC):
        out_end(j)
    in_end(0)
    in_end(1)

    for m in range(3):
        rows = slice(m * 144, (m + 1) * 144)
        for lanes, ir in ((slice(0, WP), irp), (slice(WP, DI), irq)):
            acc = None
            for n in range(2):
                seq = slice(n * SEQ, (n + 1) * SEQ)
                prod = jnp.dot(orot[rows, seq], ir[seq, :], preferred_element_type=F32)
                acc = prod * prod if acc is None else acc + prod * prod
            out_ref[rows, lanes] = acc * F32(1.0 / ROWS)
    for c in sends:
        c.wait_send()


def on_device(out_grads, inputs, out_basis, in_basis):
    dma = pltpu.SemaphoreType.DMA
    vm = pltpu.VMEM
    return pl.pallas_call(
        kernel,
        out_shape=jax.ShapeDtypeStruct((DO, DI), F32),
        in_specs=[pl.BlockSpec(memory_space=pl.ANY)] * 4,
        out_specs=pl.BlockSpec(memory_space=pltpu.VMEM),
        scratch_shapes=[
            vm((ROWS, KO), BF16), vm((ROWS, KI), BF16), vm((KO, DO), BF16), vm((DO, KO), BF16),
            vm((4, DO, 256), F32), vm((4, DO, 256), F32), vm((NC, DO, TC), F32), vm((NC, DO, TC), BF16),
            vm((NC, DO, TC), BF16), vm((NC, DO, TC), BF16), vm((DO, ROWS), BF16),
            vm((KI, ROWS), BF16), vm((4 * KI, 512), BF16), vm((4 * KI, 512), BF16),
            vm((4 * KI, WP), BF16), vm((4 * KI, WQ), BF16),
            vm((NS, TS, WP), F32), vm((NS, TS, WQ), F32), vm((NS, TS, WP), RS), vm((NS, TS, WQ), RS),
            vm((NS, 3, TO, WP), RS), vm((NS, 3, TO, WQ), RS),
            vm((NS, TO, DI), F32), vm((NS, TO, DI), BF16), vm((NS, TO, DI), BF16),
            vm((ROWS, WP), BF16), vm((ROWS, WQ), BF16),
            dma((4,)), dma((4, 2)), dma((4,)), dma((4,)), dma((NC,)), dma((NC,)),
            dma((NC,)), dma((NC,)), dma((NC,)), dma((NC,)), dma((NC, 2)), dma((NC,)),
            dma((2, 2, 3)), dma((2, 2, 3)), dma((NS, 2, 3)), dma((NS, 2, 3)), dma((NS,)), dma((NS,)),
            dma((NS, 2, 3)), dma((NS, 2, 3)), dma((NS, 2, 3, 4)), dma((NS, 2, 3, 4)),
        ],
        compiler_params=pltpu.CompilerParams(
            collective_id=0, has_side_effects=True, vmem_limit_bytes=56 * 1024 * 1024
        ),
        cost_estimate=pl.CostEstimate(flops=4_600_000_000, bytes_accessed=10_600_000, transcendentals=0),
        name="correction",
    )(out_grads, inputs, out_basis, in_basis)


def solution(mesh):
    in_specs = (P(None, "col"), P(None, "row"), P("col", "row"), P("row", "col"))
    return jax.shard_map(
        on_device, mesh=mesh, in_specs=in_specs, out_specs=P("row", "col"), check_vma=False
    )
```

```python
import jax
import jax.numpy as jnp
from jax import lax
from jax.experimental import pallas as pl
from jax.experimental.pallas import tpu as pltpu
from jax.sharding import PartitionSpec as P

MESH = pl.DeviceIdType.MESH
F32 = jnp.float32
BF16 = jnp.bfloat16

ROWS = 2048
SEQ = 1024
KO = 1728
DO = 432
KI = 160
DI = 640
WP = 384
WQ = DI - WP
TC = 128
DH = 224
NC = 2 * SEQ // TC
NS = 4
TS = 512 // NS
TO = TS // 4
PEERS = (1, 3, 2)
HK = KI // 2
RS = BF16


def kernel(
    ogt_hbm, inpt_hbm, obt_hbm, ib_hbm, out_ref,
    og, obt, po, pi, ssum, sbuf, ra, rb, orot,
    xp, xq, bp, bq, fp, fq, sp, sq, rp, rq, gz, zs, zr, irp, irq,
    ld, og_sem, core_s, core_r, coreo_s, coreo_r, za_s, za_r, zb_s, zb_r, zc_s, zc_r,
    a_s, a_r, x_s, x_r, y_s, y_r, b_s, b_r, h_s, h_r, c1_s, c1_r, c2_s, c2_r, c3_s, c3_r,
):
    row = lax.axis_index("row")
    col = lax.axis_index("col")
    zh = row // 16
    x = (row // 4) % 4
    y = row % 4
    zl = col // 2
    core = col % 2
    pu = y * (1 - core) + x * core
    pv = x * (1 - core) + y * core

    def uv(du, dv):
        dy = du * (1 - core) + dv * core
        dx = dv * (1 - core) + du * core
        return (zh * 16 + ((x + dx) % 4) * 4 + (y + dy) % 4, col)

    other_core = (row, zl * 2 + 1 - core)
    partner = ((1 - zh) * 16 + x * 4 + y, col)

    def remote(src, dst, s, r, dev):
        return pltpu.make_async_remote_copy(
            src_ref=src, dst_ref=dst, send_sem=s, recv_sem=r, device_id=dev, device_id_type=MESH
        )

    def own_rows(pos):
        return pl.ds(pl.multiple_of(pos * HK, 16), HK)

    barrier = pltpu.get_barrier_semaphore()

    def greet(dev):
        pl.semaphore_signal(barrier, inc=1, device_id=dev, device_id_type=MESH)

    for d in PEERS:
        greet(uv(d, 0))
        greet(uv(0, d))
    greet(other_core)
    greet(partner)

    @pl.when(zl > 0)
    def _():
        greet((row, col - 2))

    @pl.when(zl < 3)
    def _():
        greet((row, col + 2))

    ends = jnp.where((zl == 0) | (zl == 3), 1, 0)
    sends = []

    pl.semaphore_wait(barrier, 10 - ends)

    half = pl.ds(pl.multiple_of(core * HK, 16), HK)
    axes = ((0, pu, lambda d: uv(d, 0), xp, xq, bp), (1, pv, lambda d: uv(0, d), xq, xp, bq))
    x_copies = {}
    b_blocks = []
    hand = {}

    def x_send(st):
        for i, d in enumerate(PEERS):
            for g, pos, dev, xb, _, _ in axes:
                to = pl.ds(pl.multiple_of(((pos + d) % 4) * 512 + st * TS, TS), TS)
                here = xb.at[core, own_rows(pos), pl.ds(st * TS, TS)]
                c = remote(inpt_hbm.at[half, to], here, x_s.at[st, g, i], x_r.at[st, g, i], dev(d))
                c.start()
                x_copies[st, g, i] = c
                sends.append(c)

    def x_hand(st):
        for g, pos, dev, xb, other, _ in axes:
            for i in range(3):
                x_copies[st, g, i].wait_recv()
            lanes = pl.ds(st * TS, TS)
            c = remote(xb.at[core, :, lanes], other.at[core, :, lanes], y_s.at[st, g], y_r.at[st, g], other_core)
            c.start()
            hand[st, g] = c
            sends.append(c)

    def basis_send():
        for i, d in enumerate(PEERS):
            for g, pos, dev, _, _, bb in axes:
                lanes = slice(0, WP) if g == 0 else slice(WP, DI)
                for h in range(2):
                    c = remote(
                        ib_hbm.at[h * HK:(h + 1) * HK, lanes], bb.at[h, own_rows(pos)],
                        a_s.at[g, i, h], a_r.at[g, i, h], dev(d),
                    )
                    c.start()
                    b_blocks.append(c)
                    sends.append(c)

    own_loads = []
    og_loads = {}
    ld_ob = pltpu.make_async_copy(obt_hbm, obt, ld.at[0])

    def load_own():
        for g, pos, _, xb, _, bb in axes:
            at = pl.ds(pl.multiple_of(pos * 512, 512), 512)
            lanes = slice(0, WP) if g == 0 else slice(WP, DI)
            own_loads.append(pltpu.make_async_copy(inpt_hbm.at[half, at], xb.at[core, own_rows(pos)], ld.at[1 + 3 * g]))
            for h in range(2):
                own_loads.append(
                    pltpu.make_async_copy(
                        ib_hbm.at[h * HK:(h + 1) * HK, lanes], bb.at[h, own_rows(pos)], ld.at[2 + 3 * g + h]
                    )
                )
        for c in own_loads:
            c.start()

    mine = pl.multiple_of(core * SEQ, SEQ)
    theirs = pl.multiple_of((1 - core) * SEQ, SEQ)

    def load_gradients(base, jj, k):
        at = pl.ds(pl.multiple_of(base + jj * 256, 256), 256)
        c = pltpu.make_async_copy(ogt_hbm.at[:, at], og.at[:, at], og_sem.at[jj, k])
        c.start()
        og_loads[jj, k] = c

    def out_product(base, jj, k):
        og_loads[jj, k].wait()
        g = og[:, pl.ds(pl.multiple_of(base + jj * 256, 256), 256)]
        return jnp.dot(obt[...], g, preferred_element_type=F32)

    core_copies = []

    def out_theirs(jj):
        po[jj] = out_product(theirs, jj, 0)
        c = remote(po.at[jj], pi.at[jj], core_s.at[jj], core_r.at[jj], other_core)
        c.start()
        core_copies.append(c)
        sends.append(c)

    def role(j):
        return zl if j % 2 == 0 else 3 - zl

    def step(j, by):
        return (row, col + 2 * by if j % 2 == 0 else col - 2 * by)

    def rows(j):
        return slice(0, DH) if j % 2 == 0 else slice(DH, DO)

    def za(j, by):
        return remote(
            sbuf.at[j // 2, rows(j)], ra.at[j // 2, rows(j)], za_s.at[j], za_r.at[j], step(j, by)
        )

    def zb(j):
        return remote(
            sbuf.at[j // 2, rows(j)], rb.at[j // 2, rows(j)], zb_s.at[j], zb_r.at[j], step(j, -1)
        )

    def piece(j):
        return orot.at[rows(j), pl.ds(pl.multiple_of(mine + (j // 2) * TC, TC), TC)]

    def zc(j, by, k):
        return remote(piece(j), piece(j), zc_s.at[j, k], zc_r.at[j], step(j, by))

    def co(j):
        return remote(piece(j), piece(j), coreo_s.at[j], coreo_r.at[j], other_core)

    def out_mine(jj):
        own = out_product(mine, jj, 1)
        core_copies[jj].wait_recv()
        total = own + pi[jj]
        for h in range(2):
            ssum[2 * jj + h] = total[:, h * TC:(h + 1) * TC]
            sbuf[2 * jj + h] = total[:, h * TC:(h + 1) * TC].astype(BF16)

    def out_send(j):
        p = role(j)

        @pl.when(p == 0)
        def _():
            za(j, 1).start()

        @pl.when(p == 3)
        def _():
            za(j, -1).start()

    def out_a(j):
        @pl.when(role(j) == 2)
        def _():
            za(j, 1).wait_recv()
            at = rows(j)
            sbuf[j // 2, at] = (ssum[j // 2, at] + ra[j // 2, at].astype(F32)).astype(BF16)
            zb(j).start()

    def out_b(j):
        @pl.when(role(j) == 1)
        def _():
            za(j, 1).wait_recv()
            zb(j).wait_recv()
            at = rows(j)
            total = ssum[j // 2, at] + ra[j // 2, at].astype(F32) + rb[j // 2, at].astype(F32)
            piece(j)[...] = total.astype(BF16)
            zc(j, 1, 1).start()
            zc(j, -1, 0).start()
            co(j).start()

    def out_c(j):
        @pl.when(role(j) == 2)
        def _():
            zc(j, 1, 0).wait_recv()
            zc(j, 1, 0).start()
            co(j).start()

    def out_d(j):
        p = role(j)

        @pl.when((p == 0) | (p == 3))
        def _():
            zc(j, 1, 0).wait_recv()
            co(j).start()

    def out_end(j):
        co(j).wait_recv()
        co(j).wait_send()
        p = role(j)

        @pl.when(p == 0)
        def _():
            za(j, 1).wait_send()

        @pl.when(p == 3)
        def _():
            za(j, -1).wait_send()

        @pl.when(p == 2)
        def _():
            zb(j).wait_send()
            zc(j, 1, 0).wait_send()

        @pl.when(p == 1)
        def _():
            zc(j, -1, 0).wait_send()
            zc(j, 1, 1).wait_send()

    blocks = ((0, pv, lambda d: uv(0, d), xp, bp, fp, sp, rp), (1, pu, lambda d: uv(d, 0), xq, bq, fq, sq, rq))
    b_copies = {}

    def in_partial(st):
        for g in range(2):
            hand[st, g].wait_recv()
        for g, pos, dev, xb, bb, f, s, r in blocks:
            turned = xb[:, :, st * TS:(st + 1) * TS].reshape(4 * KI, TS).T
            part = jnp.dot(turned, bb[...].reshape(4 * KI, bb.shape[-1]), preferred_element_type=F32)
            f[st] = part
            s[st] = part.astype(RS)
            for i, d in enumerate(PEERS):
                to = pl.ds(pl.multiple_of(((pos + d) % 4) * TO, TO), TO)
                c = remote(s.at[st, to], r.at[st, i], b_s.at[st, g, i], b_r.at[st, g, i], dev(d))
                c.start()
                b_copies[st, g, i] = c
                sends.append(c)

    h_copies = {}

    def in_cross(st):
        for g, pos, dev, xb, bb, f, s, r in blocks:
            for i in range(3):
                b_copies[st, g, i].wait_recv()
            total = f[st, pl.ds(pl.multiple_of(pos * TO, TO), TO), :]
            for i in range(3):
                total = total + r[st, i].astype(F32)
            lanes = slice(0, WP) if g == 0 else slice(WP, DI)
            gz[st, :, lanes] = total
            zs[st, :, lanes] = total.astype(BF16)
        c = remote(zs.at[st], zr.at[st], h_s.at[st], h_r.at[st], partner)
        c.start()
        h_copies[st] = c
        sends.append(c)

    gather = (
        (0, irp, pu, pv, lambda d: uv(d, 0), lambda d: uv(0, d)),
        (1, irq, pv, pu, lambda d: uv(0, d), lambda d: uv(d, 0)),
    )
    def sub(buf, first, second, st):
        return buf.at[pl.ds(pl.multiple_of(first * 512 + st * TS + second * TO, TO), TO)]

    c1 = {}

    def in_round(st):
        h_copies[st].wait_recv()
        for g, buf, first, second, along, across in gather:
            lanes = slice(0, WP) if g == 0 else slice(WP, DI)
            whole = gz[st, :, lanes] + zr[st, :, lanes].astype(F32)
            sub(buf, first, second, st)[...] = whole.astype(BF16)
        for g, buf, first, second, along, across in gather:
            at = sub(buf, first, second, st)
            for i, d in enumerate(PEERS):
                c = remote(at, at, c1_s.at[st, g, i], c1_r.at[st, g, i], across(d))
                c.start()
                c1[st, g, i] = c
                sends.append(c)

    c2 = {}
    c3 = {}

    def slab(buf, first, st, lo, n):
        return buf.at[pl.ds(pl.multiple_of(first * 512 + st * TS + lo, 16), n)]

    def in_spread(st):
        for g, buf, first, second, along, across in gather:
            for i in range(3):
                c1[st, g, i].wait_recv()
            at = slab(buf, first, st, 0, TS)
            for side in range(2):
                c = remote(at, at, c2_s.at[st, g, side], c2_r.at[st, g, side], along(1 + 2 * side))
                c.start()
                c2[st, g, side] = c
                sends.append(c)

    def in_forward(st):
        for side in range(2):
            for g, buf, first, second, along, across in gather:
                c2[st, g, side].wait_recv()
                at = slab(buf, (first + 3 - 2 * side) % 4, st, side * (TS // 2), TS // 2)
                c = remote(at, at, c3_s.at[st, g, side], c3_r.at[st, g, side], along(1 + 2 * side))
                c.start()
                c3[st, g, side] = c
                sends.append(c)

    def in_end(st):
        for g in range(2):
            for side in range(2):
                c3[st, g, side].wait_recv()

    x_send(0)
    x_send(1)
    basis_send()
    x_send(2)
    ld_ob.start()
    load_gradients(theirs, 0, 0)
    load_gradients(theirs, 1, 0)
    load_gradients(mine, 0, 1)
    load_own()
    for jj, k in ((2, 0), (1, 1), (3, 0), (2, 1), (3, 1)):
        load_gradients(mine if k else theirs, jj, k)
    ld_ob.wait()
    out_theirs(0)
    out_theirs(1)
    for c in own_loads:
        c.wait()
    x_hand(0)
    out_mine(0)
    out_send(0)
    out_send(1)
    out_send(2)
    out_send(3)
    out_mine(1)
    out_send(4)
    out_theirs(2)
    out_a(0)
    for c in b_blocks:
        c.wait_recv()
    in_partial(0)
    out_a(1)
    out_send(5)
    x_hand(1)
    out_mine(2)
    out_b(0)
    x_send(3)
    out_send(6)
    out_a(2)
    x_hand(2)
    out_b(1)
    out_send(7)
    out_a(3)
    in_partial(1)
    in_cross(0)
    out_send(8)
    out_a(4)
    in_partial(2)
    x_hand(3)
    out_c(0)
    out_b(2)
    out_c(1)
    in_cross(1)
    out_b(3)
    out_a(5)
    out_send(9)
    out_a(6)
    in_partial(3)
    out_c(2)
    out_a(7)
    out_b(4)
    in_cross(2)
    out_send(10)
    out_theirs(3)
    out_a(8)
    out_send(11)
    in_round(0)
    in_cross(3)
    out_b(5)
    out_c(3)
    out_mine(3)
    out_b(6)
    in_round(1)
    out_b(7)
    out_d(0)
    out_send(12)
    in_spread(0)
    out_a(9)
    out_a(10)
    out_b(8)
    out_d(1)
    in_round(2)
    in_spread(1)
    out_c(4)
    out_c(5)
    out_a(11)
    out_d(2)
    in_round(3)
    out_c(6)
    out_send(13)
    out_d(3)
    in_spread(2)
    out_send(14)
    out_send(15)
    out_c(7)
    in_forward(0)
    out_b(9)
    out_c(8)
    out_a(12)
    out_b(10)
    out_d(4)
    out_b(11)
    out_d(5)
    out_a(13)
    out_d(6)
    out_d(7)
    in_spread(3)
    out_c(9)
    out_a(14)
    out_c(10)
    out_a(15)
    in_forward(1)
    out_d(8)
    out_b(12)
    in_forward(2)
    out_c(11)
    out_b(13)
    in_forward(3)
    out_b(14)
    out_b(15)
    out_d(9)
    out_d(10)
    out_c(12)
    out_d(11)
    out_d(12)
    out_d(13)
    out_c(13)
    out_c(14)
    out_d(14)
    out_c(15)
    out_d(15)
    for j in range(NC):
        out_end(j)
    for st in range(NS):
        in_end(st)

    for m in range(3):
        part = slice(m * 144, (m + 1) * 144)
        for lanes, ir in ((slice(0, WP), irp), (slice(WP, DI), irq)):
            acc = None
            for n in range(2):
                seq = slice(n * SEQ, (n + 1) * SEQ)
                prod = jnp.dot(orot[part, seq], ir[seq, :], preferred_element_type=F32)
                acc = prod * prod if acc is None else acc + prod * prod
            out_ref[part, lanes] = acc * F32(1.0 / ROWS)
    for c in sends:
        c.wait_send()


def settle(src, dst, go):
    c = pltpu.make_async_copy(src, dst, go)
    c.start()
    c.wait()


def on_device(out_grads, inputs, out_basis, in_basis):
    dma = pltpu.SemaphoreType.DMA
    vm = pltpu.VMEM
    result = pl.pallas_call(
        kernel,
        out_shape=pltpu.VMEM((DO, DI), F32),
        in_specs=[pl.BlockSpec(memory_space=pl.ANY)] * 4,
        out_specs=pl.BlockSpec(memory_space=pltpu.VMEM),
        scratch_shapes=[
            vm((KO, ROWS), BF16), vm((DO, KO), BF16),
            vm((4, DO, 256), F32), vm((4, DO, 256), F32), vm((NC // 2, DO, TC), F32), vm((NC // 2, DO, TC), BF16),
            vm((NC // 2, DO, TC), BF16), vm((NC // 2, DO, TC), BF16), vm((DO, ROWS), BF16),
            vm((2, 4 * HK, 512), BF16), vm((2, 4 * HK, 512), BF16),
            vm((2, 4 * HK, WP), BF16), vm((2, 4 * HK, WQ), BF16),
            vm((NS, TS, WP), F32), vm((NS, TS, WQ), F32), vm((NS, TS, WP), RS), vm((NS, TS, WQ), RS),
            vm((NS, 3, TO, WP), RS), vm((NS, 3, TO, WQ), RS),
            vm((NS, TO, DI), F32), vm((NS, TO, DI), BF16), vm((NS, TO, DI), BF16),
            vm((ROWS, WP), BF16), vm((ROWS, WQ), BF16),
            dma((8,)), dma((4, 2)), dma((4,)), dma((4,)), dma((NC,)), dma((NC,)),
            dma((NC,)), dma((NC,)), dma((NC,)), dma((NC,)), dma((NC, 2)), dma((NC,)),
            dma((2, 3, 2)), dma((2, 3, 2)), dma((NS, 2, 3)), dma((NS, 2, 3)), dma((NS, 2)), dma((NS, 2)),
            dma((NS, 2, 3)), dma((NS, 2, 3)), dma((NS,)), dma((NS,)),
            dma((NS, 2, 3)), dma((NS, 2, 3)), dma((NS, 2, 2)), dma((NS, 2, 2)), dma((NS, 2, 2)), dma((NS, 2, 2)),
        ],
        compiler_params=pltpu.CompilerParams(
            collective_id=0, has_side_effects=True, vmem_limit_bytes=56 * 1024 * 1024
        ),
        cost_estimate=pl.CostEstimate(flops=4_600_000_000, bytes_accessed=10_600_000, transcendentals=0),
        name="correction",
    )(out_grads.T, inputs.T, out_basis.T, in_basis)
    return pl.pallas_call(
        settle,
        out_shape=jax.ShapeDtypeStruct((DO, DI), F32),
        in_specs=[pl.BlockSpec(memory_space=pltpu.VMEM)],
        out_specs=pl.BlockSpec(memory_space=pl.ANY),
        scratch_shapes=[dma],
        name="settle",
    )(pltpu.with_memory_space_constraint(result, pltpu.VMEM))


def solution(mesh):
    in_specs = (P(None, "col"), P(None, "row"), P("col", "row"), P("row", "col"))
    return jax.shard_map(
        on_device, mesh=mesh, in_specs=in_specs, out_specs=P("row", "col"), check_vma=False
    )
```

```python
import jax
import jax.numpy as jnp
from jax import lax
from jax.experimental import pallas as pl
from jax.experimental.pallas import tpu as pltpu
from jax.sharding import PartitionSpec as P

MESH = pl.DeviceIdType.MESH
F32 = jnp.float32
BF16 = jnp.bfloat16

ROWS = 2048
SEQ = 1024
KO = 1728
DO = 432
KI = 160
DI = 640
WP = 384
WQ = DI - WP
TC = 128
DH = 224
NC = 2 * SEQ // TC
STRAIGHT = range(NC - 4, NC)
NS = 4
TS = 512 // NS
TO = TS // 4
PEERS = (1, 3, 2)
HK = KI // 2
RS = BF16


def kernel(
    ogt_hbm, inpt_hbm, obt_hbm, ib_hbm, orot, irp, irq,
    og, obt, po, pi, ssum, sbuf, ra, rb,
    xp, xq, turned, bp, bq, fp, fq, sp, sq, rp, rq, gz, zs, zr,
    ld, og_sem, core_s, core_r, coreo_s, coreo_r, za_s, za_r, zb_s, zb_r, zc_s, zc_r,
    a_s, a_r, x_s, x_r, y_s, y_r, b_s, b_r, h_s, h_r, c1_s, c1_r, c2_s, c2_r, c3_s, c3_r,
):
    row = lax.axis_index("row")
    col = lax.axis_index("col")
    zh = row // 16
    x = (row // 4) % 4
    y = row % 4
    zl = col // 2
    core = col % 2
    pu = y * (1 - core) + x * core
    pv = x * (1 - core) + y * core

    def uv(du, dv):
        dy = du * (1 - core) + dv * core
        dx = dv * (1 - core) + du * core
        return (zh * 16 + ((x + dx) % 4) * 4 + (y + dy) % 4, col)

    other_core = (row, zl * 2 + 1 - core)
    partner = ((1 - zh) * 16 + x * 4 + y, col)

    def remote(src, dst, s, r, dev):
        return pltpu.make_async_remote_copy(
            src_ref=src, dst_ref=dst, send_sem=s, recv_sem=r, device_id=dev, device_id_type=MESH
        )

    def own_rows(pos):
        return pl.ds(pl.multiple_of(pos * HK, 16), HK)

    barrier = pltpu.get_barrier_semaphore()

    def greet(dev):
        pl.semaphore_signal(barrier, inc=1, device_id=dev, device_id_type=MESH)

    for d in PEERS:
        greet(uv(d, 0))
        greet(uv(0, d))
    greet(other_core)
    greet(partner)
    greet((row, (col + 4) % 8))

    @pl.when(zl > 0)
    def _():
        greet((row, col - 2))

    @pl.when(zl < 3)
    def _():
        greet((row, col + 2))

    ends = jnp.where((zl == 0) | (zl == 3), 1, 0)
    sends = []

    half = pl.ds(pl.multiple_of(core * HK, 16), HK)
    axes = ((0, pu, lambda d: uv(d, 0), xp, xq, bp), (1, pv, lambda d: uv(0, d), xq, xp, bq))
    x_copies = {}
    b_blocks = []
    hand = {}

    def x_send(st):
        for i, d in enumerate(PEERS):
            for g, pos, dev, xb, _, _ in axes:
                to = pl.ds(pl.multiple_of(((pos + d) % 4) * 512 + st * TS, TS), TS)
                here = xb.at[core, own_rows(pos), pl.ds(st * TS, TS)]
                c = remote(inpt_hbm.at[half, to], here, x_s.at[st, g, i], x_r.at[st, g, i], dev(d))
                c.start()
                x_copies[st, g, i] = c
                sends.append(c)

    def x_hand(st):
        for g, pos, dev, xb, other, _ in axes:
            for i in range(3):
                x_copies[st, g, i].wait_recv()
            lanes = pl.ds(st * TS, TS)
            c = remote(xb.at[core, :, lanes], other.at[core, :, lanes], y_s.at[st, g], y_r.at[st, g], other_core)
            c.start()
            hand[st, g] = c
            sends.append(c)

    def basis_send():
        for i, d in enumerate(PEERS):
            for g, pos, dev, _, _, bb in axes:
                lanes = slice(0, WP) if g == 0 else slice(WP, DI)
                for h in range(2):
                    c = remote(
                        ib_hbm.at[h * HK:(h + 1) * HK, lanes], bb.at[h, own_rows(pos)],
                        a_s.at[g, i, h], a_r.at[g, i, h], dev(d),
                    )
                    c.start()
                    b_blocks.append(c)
                    sends.append(c)

    own_loads = []
    og_loads = {}
    ld_ob = pltpu.make_async_copy(obt_hbm, obt, ld.at[0])

    def load_own():
        for g, pos, _, xb, _, bb in axes:
            at = pl.ds(pl.multiple_of(pos * 512, 512), 512)
            lanes = slice(0, WP) if g == 0 else slice(WP, DI)
            own_loads.append(pltpu.make_async_copy(inpt_hbm.at[half, at], xb.at[core, own_rows(pos)], ld.at[1 + 3 * g]))
            for h in range(2):
                own_loads.append(
                    pltpu.make_async_copy(
                        ib_hbm.at[h * HK:(h + 1) * HK, lanes], bb.at[h, own_rows(pos)], ld.at[2 + 3 * g + h]
                    )
                )
        for c in own_loads:
            c.start()

    mine = pl.multiple_of(core * SEQ, SEQ)
    theirs = pl.multiple_of((1 - core) * SEQ, SEQ)

    def load_gradients(base, jj, k):
        at = pl.ds(pl.multiple_of(base + jj * 256, 256), 256)
        c = pltpu.make_async_copy(ogt_hbm.at[:, at], og.at[k, jj], og_sem.at[jj, k])
        c.start()
        og_loads[jj, k] = c

    def out_product(jj, k):
        og_loads[jj, k].wait()
        return jnp.dot(obt[...], og[k, jj], preferred_element_type=F32)

    core_copies = []

    def out_theirs(jj):
        po[jj] = out_product(jj, 0)
        c = remote(po.at[jj], pi.at[jj], core_s.at[jj], core_r.at[jj], other_core)
        c.start()
        core_copies.append(c)
        sends.append(c)

    def role(j):
        return zl if j % 2 == 0 else 3 - zl

    def step(j, by):
        return (row, (col + 2 * by) % 8 if j % 2 == 0 else (col + 8 - 2 * by) % 8)

    def rows(j):
        return slice(0, DH) if j % 2 == 0 else slice(DH, DO)

    def za(j, by):
        return remote(
            sbuf.at[j // 2, rows(j)], ra.at[j // 2, rows(j)], za_s.at[j], za_r.at[j], step(j, by)
        )

    def zb(j):
        return remote(
            sbuf.at[j // 2, rows(j)], rb.at[j // 2, rows(j)], zb_s.at[j], zb_r.at[j], step(j, -1)
        )

    def piece(j):
        return orot.at[rows(j), pl.ds(pl.multiple_of(mine + (j // 2) * TC, TC), TC)]

    def zc(j, by, k):
        return remote(piece(j), piece(j), zc_s.at[j, k], zc_r.at[j], step(j, by))

    def co(j):
        return remote(piece(j), piece(j), coreo_s.at[j], coreo_r.at[j], other_core)

    def out_mine(jj):
        own = out_product(jj, 1)
        core_copies[jj].wait_recv()
        total = own + pi[jj]
        for h in range(2):
            ssum[2 * jj + h] = total[:, h * TC:(h + 1) * TC]
            sbuf[2 * jj + h] = total[:, h * TC:(h + 1) * TC].astype(BF16)

    def out_send(j):
        p = role(j)

        @pl.when(p == 0)
        def _():
            za(j, 1).start()

        @pl.when(p == 3)
        def _():
            za(j, -1).start()

    def out_a(j):
        @pl.when(role(j) == 2)
        def _():
            za(j, 1).wait_recv()
            at = rows(j)
            sbuf[j // 2, at] = (ssum[j // 2, at] + ra[j // 2, at].astype(F32)).astype(BF16)
            zb(j).start()

    def out_b(j):
        @pl.when(role(j) == 1)
        def _():
            za(j, 1).wait_recv()
            zb(j).wait_recv()
            at = rows(j)
            total = ssum[j // 2, at] + ra[j // 2, at].astype(F32) + rb[j // 2, at].astype(F32)
            piece(j)[...] = total.astype(BF16)
            zc(j, 1, 1).start()
            if j in STRAIGHT:
                zc(j, 2, 2).start()
            zc(j, -1, 0).start()
            co(j).start()

    def out_c(j):
        @pl.when(role(j) == 2)
        def _():
            zc(j, 1, 0).wait_recv()
            if j not in STRAIGHT:
                zc(j, 1, 0).start()
            co(j).start()

    def out_d(j):
        p = role(j)

        @pl.when((p == 0) | (p == 3))
        def _():
            zc(j, 1, 0).wait_recv()
            co(j).start()

    def out_end(j):
        co(j).wait_recv()
        co(j).wait_send()
        p = role(j)

        @pl.when(p == 0)
        def _():
            za(j, 1).wait_send()

        @pl.when(p == 3)
        def _():
            za(j, -1).wait_send()

        @pl.when(p == 2)
        def _():
            zb(j).wait_send()
            if j not in STRAIGHT:
                zc(j, 1, 0).wait_send()

        @pl.when(p == 1)
        def _():
            zc(j, -1, 0).wait_send()
            zc(j, 1, 1).wait_send()
            if j in STRAIGHT:
                zc(j, 2, 2).wait_send()

    blocks = ((0, pv, lambda d: uv(0, d), xp, bp, fp, sp, rp), (1, pu, lambda d: uv(d, 0), xq, bq, fq, sq, rq))
    b_copies = {}

    def in_turn(st):
        for g in range(2):
            hand[st, g].wait_recv()
        for g, pos, dev, xb, bb, f, s, r in blocks:
            turned[st, g] = xb[:, :, st * TS:(st + 1) * TS].reshape(4 * KI, TS).T

    def in_partial(st):
        for g, pos, dev, xb, bb, f, s, r in blocks:
            part = jnp.dot(turned[st, g], bb[...].reshape(4 * KI, bb.shape[-1]), preferred_element_type=F32)
            f[st] = part
            s[st] = part.astype(RS)
            for i, d in enumerate(PEERS):
                to = pl.ds(pl.multiple_of(((pos + d) % 4) * TO, TO), TO)
                c = remote(s.at[st, to], r.at[st, i], b_s.at[st, g, i], b_r.at[st, g, i], dev(d))
                c.start()
                b_copies[st, g, i] = c
                sends.append(c)

    h_copies = {}

    def in_cross(st):
        for g, pos, dev, xb, bb, f, s, r in blocks:
            for i in range(3):
                b_copies[st, g, i].wait_recv()
            total = f[st, pl.ds(pl.multiple_of(pos * TO, TO), TO), :]
            for i in range(3):
                total = total + r[st, i].astype(F32)
            lanes = slice(0, WP) if g == 0 else slice(WP, DI)
            gz[st, :, lanes] = total
            zs[st, :, lanes] = total.astype(BF16)
        c = remote(zs.at[st], zr.at[st], h_s.at[st], h_r.at[st], partner)
        c.start()
        h_copies[st] = c
        sends.append(c)

    gather = (
        (0, irp, pu, pv, lambda d: uv(d, 0), lambda d: uv(0, d)),
        (1, irq, pv, pu, lambda d: uv(0, d), lambda d: uv(d, 0)),
    )
    def sub(buf, first, second, st):
        return buf.at[pl.ds(pl.multiple_of(first * 512 + st * TS + second * TO, TO), TO)]

    c1 = {}

    def in_round(st):
        h_copies[st].wait_recv()
        for g, buf, first, second, along, across in gather:
            lanes = slice(0, WP) if g == 0 else slice(WP, DI)
            whole = gz[st, :, lanes] + zr[st, :, lanes].astype(F32)
            sub(buf, first, second, st)[...] = whole.astype(BF16)
        for g, buf, first, second, along, across in gather:
            at = sub(buf, first, second, st)
            for i, d in enumerate(PEERS):
                c = remote(at, at, c1_s.at[st, g, i], c1_r.at[st, g, i], across(d))
                c.start()
                c1[st, g, i] = c
                sends.append(c)

    c2 = {}
    c3 = {}

    def slab(buf, first, st, lo, n):
        return buf.at[pl.ds(pl.multiple_of(first * 512 + st * TS + lo, 16), n)]

    def in_spread(st):
        for g, buf, first, second, along, across in gather:
            for i in range(3):
                c1[st, g, i].wait_recv()
            at = slab(buf, first, st, 0, TS)
            for side, d in enumerate(PEERS if st == NS - 1 else PEERS[:2]):
                c = remote(at, at, c2_s.at[st, g, side], c2_r.at[st, g, side], along(d))
                c.start()
                c2[st, g, side] = c
                sends.append(c)

    def in_forward(st):
        for side in range(2) if st < NS - 1 else ():
            for g, buf, first, second, along, across in gather:
                c2[st, g, side].wait_recv()
                at = slab(buf, (first + 3 - 2 * side) % 4, st, side * (TS // 2), TS // 2)
                c = remote(at, at, c3_s.at[st, g, side], c3_r.at[st, g, side], along(1 + 2 * side))
                c.start()
                c3[st, g, side] = c
                sends.append(c)

    def in_end(st):
        for g in range(2):
            if st < NS - 1:
                for side in range(2):
                    c3[st, g, side].wait_recv()
            else:
                for side in range(3):
                    c2[st, g, side].wait_recv()

    ld_ob.start()
    load_gradients(theirs, 0, 0)
    pl.semaphore_wait(barrier, 11 - ends)
    x_send(0)
    x_send(1)
    basis_send()
    load_gradients(theirs, 1, 0)
    load_gradients(mine, 0, 1)
    load_own()
    for jj, k in ((2, 0), (1, 1), (3, 0), (2, 1), (3, 1)):
        load_gradients(mine if k else theirs, jj, k)
    ld_ob.wait()
    out_theirs(0)
    x_send(2)
    x_send(3)
    out_theirs(1)
    out_mine(0)
    out_send(0)
    out_send(1)
    out_send(2)
    out_theirs(2)
    for c in own_loads:
        c.wait()
    x_hand(0)
    x_hand(1)
    out_send(3)
    out_mine(1)
    out_send(4)
    out_a(0)
    in_turn(0)
    for c in b_blocks:
        c.wait_recv()
    in_partial(0)
    x_hand(2)
    out_a(1)
    in_turn(1)
    out_send(5)
    out_send(6)
    in_partial(1)
    out_b(0)
    out_a(2)
    in_turn(2)
    x_hand(3)
    out_a(3)
    out_a(4)
    out_send(7)
    in_partial(2)
    in_cross(0)
    in_turn(3)
    in_partial(3)
    in_cross(1)
    out_mine(2)
    out_b(1)
    out_b(2)
    out_a(5)
    out_send(8)
    out_c(0)
    out_send(9)
    out_b(3)
    out_a(6)
    out_b(4)
    in_cross(2)
    out_send(10)
    out_theirs(3)
    out_a(7)
    out_send(11)
    in_cross(3)
    out_c(1)
    out_a(8)
    out_a(9)
    out_b(5)
    in_round(0)
    out_mine(3)
    out_c(2)
    out_b(6)
    out_send(12)
    out_send(13)
    out_c(3)
    out_send(14)
    out_d(0)
    out_c(4)
    out_a(10)
    in_round(1)
    out_b(7)
    in_spread(0)
    out_a(11)
    out_send(15)
    out_b(8)
    in_round(2)
    out_a(12)
    out_c(5)
    in_round(3)
    out_d(1)
    in_spread(1)
    out_b(9)
    out_d(2)
    out_d(3)
    out_d(4)
    out_a(13)
    in_forward(0)
    out_c(6)
    out_b(10)
    out_a(14)
    out_c(7)
    out_a(15)
    out_b(11)
    in_spread(2)
    out_b(12)
    out_c(8)
    in_spread(3)
    out_b(13)
    out_d(5)
    out_c(9)
    in_forward(1)
    out_d(6)
    out_c(10)
    out_d(7)
    out_b(14)
    out_b(15)
    in_forward(2)
    out_c(11)
    out_d(8)
    out_d(9)
    out_c(12)
    out_c(13)
    in_forward(3)
    out_d(10)
    out_d(11)
    out_d(12)
    out_d(13)
    out_d(14)
    out_c(14)
    out_d(15)
    out_c(15)
    for j in range(NC):
        out_end(j)
    for st in range(NS):
        in_end(st)

    for c in sends:
        c.wait_send()


def correct(orot, irp, irq, out_hbm, held, sem):
    stores = []
    for m in range(3):
        part = slice(m * 144, (m + 1) * 144)
        for lanes, ir in ((slice(0, WP), irp), (slice(WP, DI), irq)):
            acc = None
            for n in range(2):
                seq = slice(n * SEQ, (n + 1) * SEQ)
                prod = jnp.dot(orot[part, seq], ir[seq, :], preferred_element_type=F32)
                acc = prod * prod if acc is None else acc + prod * prod
            held[part, lanes] = acc * F32(1.0 / ROWS)
        c = pltpu.make_async_copy(held.at[part], out_hbm.at[part], sem.at[m])
        c.start()
        stores.append(c)
    for c in stores:
        c.wait()


def on_device(out_grads, inputs, out_basis, in_basis):
    dma = pltpu.SemaphoreType.DMA
    vm = pltpu.VMEM
    result = pl.pallas_call(
        kernel,
        out_shape=(vm((DO, ROWS), BF16), vm((ROWS, WP), BF16), vm((ROWS, WQ), BF16)),
        in_specs=[pl.BlockSpec(memory_space=pl.ANY)] * 4,
        out_specs=[pl.BlockSpec(memory_space=pltpu.VMEM)] * 3,
        scratch_shapes=[
            vm((2, 4, KO, 256), BF16), vm((DO, KO), BF16),
            vm((4, DO, 256), F32), vm((4, DO, 256), F32), vm((NC // 2, DO, TC), F32), vm((NC // 2, DO, TC), BF16),
            vm((NC // 2, DO, TC), BF16), vm((NC // 2, DO, TC), BF16),
            vm((2, 4 * HK, 512), BF16), vm((2, 4 * HK, 512), BF16), vm((NS, 2, TS, 4 * KI), BF16),
            vm((2, 4 * HK, WP), BF16), vm((2, 4 * HK, WQ), BF16),
            vm((NS, TS, WP), F32), vm((NS, TS, WQ), F32), vm((NS, TS, WP), RS), vm((NS, TS, WQ), RS),
            vm((NS, 3, TO, WP), RS), vm((NS, 3, TO, WQ), RS),
            vm((NS, TO, DI), F32), vm((NS, TO, DI), BF16), vm((NS, TO, DI), BF16),
            dma((8,)), dma((4, 2)), dma((4,)), dma((4,)), dma((NC,)), dma((NC,)),
            dma((NC,)), dma((NC,)), dma((NC,)), dma((NC,)), dma((NC, 3)), dma((NC,)),
            dma((2, 3, 2)), dma((2, 3, 2)), dma((NS, 2, 3)), dma((NS, 2, 3)), dma((NS, 2)), dma((NS, 2)),
            dma((NS, 2, 3)), dma((NS, 2, 3)), dma((NS,)), dma((NS,)),
            dma((NS, 2, 3)), dma((NS, 2, 3)), dma((NS, 2, 3)), dma((NS, 2, 3)), dma((NS, 2, 2)), dma((NS, 2, 2)),
        ],
        compiler_params=pltpu.CompilerParams(
            collective_id=0, has_side_effects=True, vmem_limit_bytes=56 * 1024 * 1024
        ),
        cost_estimate=pl.CostEstimate(flops=4_600_000_000, bytes_accessed=10_600_000, transcendentals=0),
        name="correction",
    )(out_grads.T, inputs.T, out_basis.T, in_basis)
    return pl.pallas_call(
        correct,
        out_shape=jax.ShapeDtypeStruct((DO, DI), F32),
        in_specs=[pl.BlockSpec(memory_space=pltpu.VMEM)] * 3,
        out_specs=pl.BlockSpec(memory_space=pl.ANY),
        scratch_shapes=[vm((DO, DI), F32), dma((3,))],
        compiler_params=pltpu.CompilerParams(vmem_limit_bytes=48 * 1024 * 1024),
        name="correct",
    )(*(pltpu.with_memory_space_constraint(r, pltpu.VMEM) for r in result))


def solution(mesh):
    in_specs = (P(None, "col"), P(None, "row"), P("col", "row"), P("row", "col"))
    return jax.shard_map(
        on_device, mesh=mesh, in_specs=in_specs, out_specs=P("row", "col"), check_vma=False
    )
```

```python
import jax
import jax.numpy as jnp
from jax import lax
from jax.experimental import pallas as pl
from jax.experimental.pallas import tpu as pltpu
from jax.sharding import PartitionSpec as P

MESH = pl.DeviceIdType.MESH
F32 = jnp.float32
BF16 = jnp.bfloat16

ROWS = 2048
SEQ = 1024
KO = 1728
DO = 432
KI = 160
DI = 640
WP = 384
WQ = DI - WP
TC = 128
DH = 224
NC = 2 * SEQ // TC
STRAIGHT = range(NC - 4, NC)
NS = 4
TS = 512 // NS
TO = TS // 4
PEERS = (1, 3, 2)
HK = KI // 2
RS = BF16


def kernel(
    ogt_hbm, inpt_hbm, obt_hbm, ib_hbm, orot, irp, irq,
    og, obt, po, pi, ssum, sbuf, ra, rb,
    xp, xq, turned, bp, bq, fp, fq, sp, sq, rp, rq, gz, zs, zr,
    ld, og_sem, core_s, core_r, coreo_s, coreo_r, za_s, za_r, zb_s, zb_r, zc_s, zc_r,
    a_s, a_r, x_s, x_r, y_s, y_r, b_s, b_r, h_s, h_r, c1_s, c1_r, c2_s, c2_r, c3_s, c3_r,
):
    row = lax.axis_index("row")
    col = lax.axis_index("col")
    zh = row // 16
    x = (row // 4) % 4
    y = row % 4
    zl = col // 2
    core = col % 2
    pu = y * (1 - core) + x * core
    pv = x * (1 - core) + y * core

    def uv(du, dv):
        dy = du * (1 - core) + dv * core
        dx = dv * (1 - core) + du * core
        return (zh * 16 + ((x + dx) % 4) * 4 + (y + dy) % 4, col)

    other_core = (row, zl * 2 + 1 - core)
    partner = ((1 - zh) * 16 + x * 4 + y, col)

    def remote(src, dst, s, r, dev):
        return pltpu.make_async_remote_copy(
            src_ref=src, dst_ref=dst, send_sem=s, recv_sem=r, device_id=dev, device_id_type=MESH
        )

    def own_rows(pos):
        return pl.ds(pl.multiple_of(pos * HK, 16), HK)

    barrier = pltpu.get_barrier_semaphore()

    def greet(dev):
        pl.semaphore_signal(barrier, inc=1, device_id=dev, device_id_type=MESH)

    for d in PEERS:
        greet(uv(d, 0))
        greet(uv(0, d))
    greet(other_core)
    greet(partner)
    greet((row, (col + 4) % 8))

    @pl.when(zl > 0)
    def _():
        greet((row, col - 2))

    @pl.when(zl < 3)
    def _():
        greet((row, col + 2))

    ends = jnp.where((zl == 0) | (zl == 3), 1, 0)
    sends = []

    half = pl.ds(pl.multiple_of(core * HK, 16), HK)
    axes = ((0, pu, lambda d: uv(d, 0), xp, xq, bp), (1, pv, lambda d: uv(0, d), xq, xp, bq))
    x_copies = {}
    b_blocks = []
    hand = {}

    def x_send(st):
        for i, d in enumerate(PEERS):
            for g, pos, dev, xb, _, _ in axes:
                to = pl.ds(pl.multiple_of(((pos + d) % 4) * 512 + st * TS, TS), TS)
                here = xb.at[core, own_rows(pos), pl.ds(st * TS, TS)]
                c = remote(inpt_hbm.at[half, to], here, x_s.at[st, g, i], x_r.at[st, g, i], dev(d))
                c.start()
                x_copies[st, g, i] = c
                sends.append(c)

    def x_hand(st):
        for g, pos, dev, xb, other, _ in axes:
            for i in range(3):
                x_copies[st, g, i].wait_recv()
            lanes = pl.ds(st * TS, TS)
            c = remote(xb.at[core, :, lanes], other.at[core, :, lanes], y_s.at[st, g], y_r.at[st, g], other_core)
            c.start()
            hand[st, g] = c
            sends.append(c)

    def basis_send():
        for i, d in enumerate(PEERS):
            for g, pos, dev, _, _, bb in axes:
                lanes = slice(0, WP) if g == 0 else slice(WP, DI)
                for h in range(2):
                    c = remote(
                        ib_hbm.at[h * HK:(h + 1) * HK, lanes], bb.at[h, own_rows(pos)],
                        a_s.at[g, i, h], a_r.at[g, i, h], dev(d),
                    )
                    c.start()
                    b_blocks.append(c)
                    sends.append(c)

    own_loads = []
    og_loads = {}
    ld_ob = pltpu.make_async_copy(obt_hbm, obt, ld.at[0])

    def load_own():
        for g, pos, _, xb, _, bb in axes:
            at = pl.ds(pl.multiple_of(pos * 512, 512), 512)
            lanes = slice(0, WP) if g == 0 else slice(WP, DI)
            own_loads.append(pltpu.make_async_copy(inpt_hbm.at[half, at], xb.at[core, own_rows(pos)], ld.at[1 + 3 * g]))
            for h in range(2):
                own_loads.append(
                    pltpu.make_async_copy(
                        ib_hbm.at[h * HK:(h + 1) * HK, lanes], bb.at[h, own_rows(pos)], ld.at[2 + 3 * g + h]
                    )
                )
        for c in own_loads:
            c.start()

    mine = pl.multiple_of(core * SEQ, SEQ)
    theirs = pl.multiple_of((1 - core) * SEQ, SEQ)

    def load_gradients(base, jj, k):
        at = pl.ds(pl.multiple_of(base + jj * 256, 256), 256)
        c = pltpu.make_async_copy(ogt_hbm.at[:, at], og.at[k, jj], og_sem.at[jj, k])
        c.start()
        og_loads[jj, k] = c

    def out_product(jj, k):
        og_loads[jj, k].wait()
        return jnp.dot(obt[...], og[k, jj], preferred_element_type=F32)

    core_copies = []

    def out_theirs(jj):
        po[jj] = out_product(jj, 0)
        c = remote(po.at[jj], pi.at[jj], core_s.at[jj], core_r.at[jj], other_core)
        c.start()
        core_copies.append(c)
        sends.append(c)

    def role(j):
        return zl if j % 2 == 0 else 3 - zl

    def step(j, by):
        return (row, (col + 2 * by) % 8 if j % 2 == 0 else (col + 8 - 2 * by) % 8)

    def rows(j):
        return slice(0, DH) if j % 2 == 0 else slice(DH, DO)

    def za(j, by):
        return remote(
            sbuf.at[j // 2, rows(j)], ra.at[j // 2, rows(j)], za_s.at[j], za_r.at[j], step(j, by)
        )

    def zb(j):
        return remote(
            sbuf.at[j // 2, rows(j)], rb.at[j // 2, rows(j)], zb_s.at[j], zb_r.at[j], step(j, -1)
        )

    def piece(j):
        return orot.at[rows(j), pl.ds(pl.multiple_of(mine + (j // 2) * TC, TC), TC)]

    def zc(j, by, k):
        return remote(piece(j), piece(j), zc_s.at[j, k], zc_r.at[j], step(j, by))

    def co(j):
        return remote(piece(j), piece(j), coreo_s.at[j], coreo_r.at[j], other_core)

    def out_mine(jj):
        own = out_product(jj, 1)
        core_copies[jj].wait_recv()
        total = own + pi[jj]
        for h in range(2):
            ssum[2 * jj + h] = total[:, h * TC:(h + 1) * TC]
            sbuf[2 * jj + h] = total[:, h * TC:(h + 1) * TC].astype(BF16)

    def out_send(j):
        p = role(j)

        @pl.when(p == 0)
        def _():
            za(j, 1).start()

        @pl.when(p == 3)
        def _():
            za(j, -1).start()

    def out_a(j):
        @pl.when(role(j) == 2)
        def _():
            za(j, 1).wait_recv()
            at = rows(j)
            sbuf[j // 2, at] = (ssum[j // 2, at] + ra[j // 2, at].astype(F32)).astype(BF16)
            zb(j).start()

    def out_b(j):
        @pl.when(role(j) == 1)
        def _():
            za(j, 1).wait_recv()
            zb(j).wait_recv()
            at = rows(j)
            total = ssum[j // 2, at] + ra[j // 2, at].astype(F32) + rb[j // 2, at].astype(F32)
            piece(j)[...] = total.astype(BF16)
            zc(j, 1, 1).start()
            if j in STRAIGHT:
                zc(j, 2, 2).start()
            zc(j, -1, 0).start()
            co(j).start()

    def out_c(j):
        @pl.when(role(j) == 2)
        def _():
            zc(j, 1, 0).wait_recv()
            if j not in STRAIGHT:
                zc(j, 1, 0).start()
            co(j).start()

    def out_d(j):
        p = role(j)

        @pl.when((p == 0) | (p == 3))
        def _():
            zc(j, 1, 0).wait_recv()
            co(j).start()

    def out_end(j):
        co(j).wait_recv()
        co(j).wait_send()
        p = role(j)

        @pl.when(p == 0)
        def _():
            za(j, 1).wait_send()

        @pl.when(p == 3)
        def _():
            za(j, -1).wait_send()

        @pl.when(p == 2)
        def _():
            zb(j).wait_send()
            if j not in STRAIGHT:
                zc(j, 1, 0).wait_send()

        @pl.when(p == 1)
        def _():
            zc(j, -1, 0).wait_send()
            zc(j, 1, 1).wait_send()
            if j in STRAIGHT:
                zc(j, 2, 2).wait_send()

    blocks = ((0, pv, lambda d: uv(0, d), xp, bp, fp, sp, rp), (1, pu, lambda d: uv(d, 0), xq, bq, fq, sq, rq))
    b_copies = {}

    def in_turn(st):
        for g in range(2):
            hand[st, g].wait_recv()
        for g, pos, dev, xb, bb, f, s, r in blocks:
            turned[st, g] = xb[:, :, st * TS:(st + 1) * TS].reshape(4 * KI, TS).T

    def in_partial(st):
        for g, pos, dev, xb, bb, f, s, r in blocks:
            part = jnp.dot(turned[st, g], bb[...].reshape(4 * KI, bb.shape[-1]), preferred_element_type=F32)
            f[st] = part
            s[st] = part.astype(RS)
            for i, d in enumerate(PEERS):
                to = pl.ds(pl.multiple_of(((pos + d) % 4) * TO, TO), TO)
                c = remote(s.at[st, to], r.at[st, i], b_s.at[st, g, i], b_r.at[st, g, i], dev(d))
                c.start()
                b_copies[st, g, i] = c
                sends.append(c)

    h_copies = {}

    def in_cross(st):
        for g, pos, dev, xb, bb, f, s, r in blocks:
            for i in range(3):
                b_copies[st, g, i].wait_recv()
            total = f[st, pl.ds(pl.multiple_of(pos * TO, TO), TO), :]
            for i in range(3):
                total = total + r[st, i].astype(F32)
            lanes = slice(0, WP) if g == 0 else slice(WP, DI)
            gz[st, :, lanes] = total
            zs[st, :, lanes] = total.astype(BF16)
        c = remote(zs.at[st], zr.at[st], h_s.at[st], h_r.at[st], partner)
        c.start()
        h_copies[st] = c
        sends.append(c)

    gather = (
        (0, irp, pu, pv, lambda d: uv(d, 0), lambda d: uv(0, d)),
        (1, irq, pv, pu, lambda d: uv(0, d), lambda d: uv(d, 0)),
    )
    def sub(buf, first, second, st):
        return buf.at[pl.ds(pl.multiple_of(first * 512 + st * TS + second * TO, TO), TO)]

    c1 = {}

    def in_round(st):
        h_copies[st].wait_recv()
        for g, buf, first, second, along, across in gather:
            lanes = slice(0, WP) if g == 0 else slice(WP, DI)
            whole = gz[st, :, lanes] + zr[st, :, lanes].astype(F32)
            sub(buf, first, second, st)[...] = whole.astype(BF16)
        for g, buf, first, second, along, across in gather:
            at = sub(buf, first, second, st)
            for i, d in enumerate(PEERS):
                c = remote(at, at, c1_s.at[st, g, i], c1_r.at[st, g, i], across(d))
                c.start()
                c1[st, g, i] = c
                sends.append(c)

    c2 = {}
    c3 = {}

    def slab(buf, first, st, lo, n):
        return buf.at[pl.ds(pl.multiple_of(first * 512 + st * TS + lo, 16), n)]

    def in_spread(st):
        for g, buf, first, second, along, across in gather:
            for i in range(3):
                c1[st, g, i].wait_recv()
            at = slab(buf, first, st, 0, TS)
            for side, d in enumerate(PEERS if st == NS - 1 else PEERS[:2]):
                c = remote(at, at, c2_s.at[st, g, side], c2_r.at[st, g, side], along(d))
                c.start()
                c2[st, g, side] = c
                sends.append(c)

    def in_forward(st):
        for side in range(2) if st < NS - 1 else ():
            for g, buf, first, second, along, across in gather:
                c2[st, g, side].wait_recv()
                at = slab(buf, (first + 3 - 2 * side) % 4, st, side * (TS // 2), TS // 2)
                c = remote(at, at, c3_s.at[st, g, side], c3_r.at[st, g, side], along(1 + 2 * side))
                c.start()
                c3[st, g, side] = c
                sends.append(c)

    def in_end(st):
        for g in range(2):
            if st < NS - 1:
                for side in range(2):
                    c3[st, g, side].wait_recv()
            else:
                for side in range(3):
                    c2[st, g, side].wait_recv()

    ld_ob.start()
    load_gradients(theirs, 0, 0)
    pl.semaphore_wait(barrier, 11 - ends)
    x_send(0)
    basis_send()
    load_gradients(theirs, 1, 0)
    load_gradients(mine, 0, 1)
    load_own()
    for jj, k in ((2, 0), (1, 1), (3, 0), (2, 1), (3, 1)):
        load_gradients(mine if k else theirs, jj, k)
    ld_ob.wait()
    out_theirs(0)
    x_send(1)
    out_theirs(1)
    x_send(2)
    out_mine(0)
    out_send(0)
    out_send(1)
    for c in own_loads:
        c.wait()
    x_hand(0)
    out_send(2)
    out_send(3)
    out_theirs(2)
    out_mine(1)
    in_turn(0)
    out_a(0)
    out_send(4)
    x_send(3)
    for c in b_blocks:
        c.wait_recv()
    in_partial(0)
    out_send(5)
    out_send(6)
    out_a(1)
    x_hand(1)
    out_mine(2)
    out_a(2)
    out_a(3)
    out_b(0)
    x_hand(2)
    out_send(7)
    in_turn(1)
    out_send(8)
    out_a(4)
    in_partial(1)
    x_hand(3)
    out_b(1)
    in_cross(0)
    out_send(9)
    out_a(5)
    in_turn(2)
    in_partial(2)
    out_a(6)
    out_b(2)
    out_b(3)
    in_turn(3)
    in_partial(3)
    in_cross(1)
    out_c(0)
    out_b(4)
    out_a(7)
    in_cross(2)
    out_send(10)
    out_a(8)
    out_send(11)
    out_theirs(3)
    out_c(1)
    in_cross(3)
    out_mine(3)
    out_b(5)
    out_d(0)
    out_send(12)
    in_round(0)
    out_b(6)
    out_send(13)
    out_c(2)
    out_a(9)
    out_a(10)
    out_send(14)
    in_round(1)
    out_c(3)
    out_b(7)
    out_c(4)
    out_d(1)
    in_spread(0)
    out_d(2)
    out_a(11)
    out_send(15)
    out_a(12)
    out_b(8)
    in_round(2)
    out_b(9)
    out_a(13)
    in_round(3)
    out_c(5)
    out_b(10)
    out_c(6)
    in_spread(1)
    out_a(14)
    out_d(3)
    out_b(11)
    out_c(7)
    out_a(15)
    out_b(12)
    in_forward(0)
    out_d(4)
    out_b(13)
    in_spread(2)
    out_c(8)
    out_c(9)
    out_d(5)
    out_d(6)
    in_spread(3)
    out_b(14)
    out_c(10)
    out_c(11)
    out_d(7)
    out_b(15)
    in_forward(1)
    out_d(8)
    in_forward(2)
    out_d(9)
    out_c(12)
    out_d(10)
    out_d(11)
    out_c(13)
    out_d(12)
    out_d(13)
    out_d(14)
    out_d(15)
    out_c(14)
    out_c(15)
    in_forward(3)
    for j in range(NC):
        out_end(j)
    for st in range(NS):
        in_end(st)

    for c in sends:
        c.wait_send()


def correct(orot, irp, irq, out_hbm, held, sem):
    stores = []
    for m in range(3):
        part = slice(m * 144, (m + 1) * 144)
        for lanes, ir in ((slice(0, WP), irp), (slice(WP, DI), irq)):
            acc = None
            for n in range(2):
                seq = slice(n * SEQ, (n + 1) * SEQ)
                prod = jnp.dot(orot[part, seq], ir[seq, :], preferred_element_type=F32)
                acc = prod * prod if acc is None else acc + prod * prod
            held[part, lanes] = acc * F32(1.0 / ROWS)
        c = pltpu.make_async_copy(held.at[part], out_hbm.at[part], sem.at[m])
        c.start()
        stores.append(c)
    for c in stores:
        c.wait()


def on_device(out_grads, inputs, out_basis, in_basis):
    dma = pltpu.SemaphoreType.DMA
    vm = pltpu.VMEM
    result = pl.pallas_call(
        kernel,
        out_shape=(vm((DO, ROWS), BF16), vm((ROWS, WP), BF16), vm((ROWS, WQ), BF16)),
        in_specs=[pl.BlockSpec(memory_space=pl.ANY)] * 4,
        out_specs=[pl.BlockSpec(memory_space=pltpu.VMEM)] * 3,
        scratch_shapes=[
            vm((2, 4, KO, 256), BF16), vm((DO, KO), BF16),
            vm((4, DO, 256), F32), vm((4, DO, 256), F32), vm((NC // 2, DO, TC), F32), vm((NC // 2, DO, TC), BF16),
            vm((NC // 2, DO, TC), BF16), vm((NC // 2, DO, TC), BF16),
            vm((2, 4 * HK, 512), BF16), vm((2, 4 * HK, 512), BF16), vm((NS, 2, TS, 4 * KI), BF16),
            vm((2, 4 * HK, WP), BF16), vm((2, 4 * HK, WQ), BF16),
            vm((NS, TS, WP), F32), vm((NS, TS, WQ), F32), vm((NS, TS, WP), RS), vm((NS, TS, WQ), RS),
            vm((NS, 3, TO, WP), RS), vm((NS, 3, TO, WQ), RS),
            vm((NS, TO, DI), F32), vm((NS, TO, DI), BF16), vm((NS, TO, DI), BF16),
            dma((8,)), dma((4, 2)), dma((4,)), dma((4,)), dma((NC,)), dma((NC,)),
            dma((NC,)), dma((NC,)), dma((NC,)), dma((NC,)), dma((NC, 3)), dma((NC,)),
            dma((2, 3, 2)), dma((2, 3, 2)), dma((NS, 2, 3)), dma((NS, 2, 3)), dma((NS, 2)), dma((NS, 2)),
            dma((NS, 2, 3)), dma((NS, 2, 3)), dma((NS,)), dma((NS,)),
            dma((NS, 2, 3)), dma((NS, 2, 3)), dma((NS, 2, 3)), dma((NS, 2, 3)), dma((NS, 2, 2)), dma((NS, 2, 2)),
        ],
        compiler_params=pltpu.CompilerParams(
            collective_id=0, has_side_effects=True, vmem_limit_bytes=56 * 1024 * 1024
        ),
        cost_estimate=pl.CostEstimate(flops=4_600_000_000, bytes_accessed=10_600_000, transcendentals=0),
        name="correction",
    )(out_grads.T, inputs.T, out_basis.T, in_basis)
    return pl.pallas_call(
        correct,
        out_shape=jax.ShapeDtypeStruct((DO, DI), F32),
        in_specs=[pl.BlockSpec(memory_space=pltpu.VMEM)] * 3,
        out_specs=pl.BlockSpec(memory_space=pl.ANY),
        scratch_shapes=[vm((DO, DI), F32), dma((3,))],
        compiler_params=pltpu.CompilerParams(vmem_limit_bytes=48 * 1024 * 1024),
        name="correct",
    )(*(pltpu.with_memory_space_constraint(r, pltpu.VMEM) for r in result))


def solution(mesh):
    in_specs = (P(None, "col"), P(None, "row"), P("col", "row"), P("row", "col"))
    return jax.shard_map(
        on_device, mesh=mesh, in_specs=in_specs, out_specs=P("row", "col"), check_vma=False
    )
```

```python
import jax
import jax.numpy as jnp
from jax import lax
from jax.experimental import pallas as pl
from jax.experimental.pallas import tpu as pltpu
from jax.sharding import PartitionSpec as P

MESH = pl.DeviceIdType.MESH
F32 = jnp.float32
BF16 = jnp.bfloat16

ROWS = 2048
SEQ = 1024
KO = 1728
DO = 432
KI = 160
DI = 640
WP = 384
WQ = DI - WP
TC = 128
DH = 224
NC = 2 * SEQ // TC
STRAIGHT = range(NC - 6, NC)
NS = 4
TS = 512 // NS
TO = TS // 4
PEERS = (1, 3, 2)
HK = KI // 2
RS = BF16


def kernel(
    ogt_hbm, inpt_hbm, obt_hbm, ib_hbm, orot, irp, irq,
    og, obt, po, pi, ssum, sbuf, ra, rb,
    xp, xq, turned, bp, bq, fp, fq, sp, sq, rp, rq, gz, zs, zr,
    ld, og_sem, core_s, core_r, coreo_s, coreo_r, za_s, za_r, zb_s, zb_r, zc_s, zc_r,
    a_s, a_r, x_s, x_r, y_s, y_r, b_s, b_r, h_s, h_r, c1_s, c1_r, c2_s, c2_r, c3_s, c3_r,
):
    row = lax.axis_index("row")
    col = lax.axis_index("col")
    zh = row // 16
    x = (row // 4) % 4
    y = row % 4
    zl = col // 2
    core = col % 2
    pu = y * (1 - core) + x * core
    pv = x * (1 - core) + y * core

    def uv(du, dv):
        dy = du * (1 - core) + dv * core
        dx = dv * (1 - core) + du * core
        return (zh * 16 + ((x + dx) % 4) * 4 + (y + dy) % 4, col)

    other_core = (row, zl * 2 + 1 - core)
    partner = ((1 - zh) * 16 + x * 4 + y, col)

    def remote(src, dst, s, r, dev):
        return pltpu.make_async_remote_copy(
            src_ref=src, dst_ref=dst, send_sem=s, recv_sem=r, device_id=dev, device_id_type=MESH
        )

    def own_rows(pos):
        return pl.ds(pl.multiple_of(pos * HK, 16), HK)

    barrier = pltpu.get_barrier_semaphore()

    def greet(dev):
        pl.semaphore_signal(barrier, inc=1, device_id=dev, device_id_type=MESH)

    for d in PEERS:
        greet(uv(d, 0))
        greet(uv(0, d))
    greet(other_core)
    greet(partner)
    greet((row, (col + 4) % 8))

    @pl.when(zl > 0)
    def _():
        greet((row, col - 2))

    @pl.when(zl < 3)
    def _():
        greet((row, col + 2))

    ends = jnp.where((zl == 0) | (zl == 3), 1, 0)
    sends = []

    half = pl.ds(pl.multiple_of(core * HK, 16), HK)
    axes = ((0, pu, lambda d: uv(d, 0), xp, xq, bp), (1, pv, lambda d: uv(0, d), xq, xp, bq))
    x_copies = {}
    b_blocks = []
    hand = {}

    def x_send(st):
        for i, d in enumerate(PEERS):
            for g, pos, dev, xb, _, _ in axes:
                to = pl.ds(pl.multiple_of(((pos + d) % 4) * 512 + st * TS, TS), TS)
                here = xb.at[core, own_rows(pos), pl.ds(st * TS, TS)]
                c = remote(inpt_hbm.at[half, to], here, x_s.at[st, g, i], x_r.at[st, g, i], dev(d))
                c.start()
                x_copies[st, g, i] = c
                sends.append(c)

    def x_hand(st):
        for g, pos, dev, xb, other, _ in axes:
            for i in range(3):
                x_copies[st, g, i].wait_recv()
            lanes = pl.ds(st * TS, TS)
            c = remote(xb.at[core, :, lanes], other.at[core, :, lanes], y_s.at[st, g], y_r.at[st, g], other_core)
            c.start()
            hand[st, g] = c
            sends.append(c)

    def basis_send():
        for i, d in enumerate(PEERS):
            for g, pos, dev, _, _, bb in axes:
                lanes = slice(0, WP) if g == 0 else slice(WP, DI)
                for h in range(2):
                    c = remote(
                        ib_hbm.at[h * HK:(h + 1) * HK, lanes], bb.at[h, own_rows(pos)],
                        a_s.at[g, i, h], a_r.at[g, i, h], dev(d),
                    )
                    c.start()
                    b_blocks.append(c)
                    sends.append(c)

    own_loads = []
    og_loads = {}
    ld_ob = pltpu.make_async_copy(obt_hbm, obt, ld.at[0])

    def load_own():
        for g, pos, _, xb, _, bb in axes:
            at = pl.ds(pl.multiple_of(pos * 512, 512), 512)
            lanes = slice(0, WP) if g == 0 else slice(WP, DI)
            own_loads.append(pltpu.make_async_copy(inpt_hbm.at[half, at], xb.at[core, own_rows(pos)], ld.at[1 + 3 * g]))
            for h in range(2):
                own_loads.append(
                    pltpu.make_async_copy(
                        ib_hbm.at[h * HK:(h + 1) * HK, lanes], bb.at[h, own_rows(pos)], ld.at[2 + 3 * g + h]
                    )
                )
        for c in own_loads:
            c.start()

    mine = pl.multiple_of(core * SEQ, SEQ)
    theirs = pl.multiple_of((1 - core) * SEQ, SEQ)

    def load_gradients(base, jj, k):
        at = pl.ds(pl.multiple_of(base + jj * 256, 256), 256)
        c = pltpu.make_async_copy(ogt_hbm.at[:, at], og.at[k, jj], og_sem.at[jj, k])
        c.start()
        og_loads[jj, k] = c

    def out_product(jj, k):
        og_loads[jj, k].wait()
        return jnp.dot(obt[...], og[k, jj], preferred_element_type=F32)

    core_copies = []

    def out_theirs(jj):
        po[jj] = out_product(jj, 0)
        c = remote(po.at[jj], pi.at[jj], core_s.at[jj], core_r.at[jj], other_core)
        c.start()
        core_copies.append(c)
        sends.append(c)

    def role(j):
        return zl if j % 2 == 0 else 3 - zl

    def step(j, by):
        return (row, (col + 2 * by) % 8 if j % 2 == 0 else (col + 8 - 2 * by) % 8)

    def rows(j):
        return slice(0, DH) if j % 2 == 0 else slice(DH, DO)

    def za(j, by):
        return remote(
            sbuf.at[j // 2, rows(j)], ra.at[j // 2, rows(j)], za_s.at[j], za_r.at[j], step(j, by)
        )

    def zb(j):
        return remote(
            sbuf.at[j // 2, rows(j)], rb.at[j // 2, rows(j)], zb_s.at[j], zb_r.at[j], step(j, -1)
        )

    def piece(j):
        return orot.at[rows(j), pl.ds(pl.multiple_of(mine + (j // 2) * TC, TC), TC)]

    def zc(j, by, k):
        return remote(piece(j), piece(j), zc_s.at[j, k], zc_r.at[j], step(j, by))

    def co(j):
        return remote(piece(j), piece(j), coreo_s.at[j], coreo_r.at[j], other_core)

    def out_mine(jj):
        own = out_product(jj, 1)
        core_copies[jj].wait_recv()
        total = own + pi[jj]
        for h in range(2):
            ssum[2 * jj + h] = total[:, h * TC:(h + 1) * TC]
            sbuf[2 * jj + h] = total[:, h * TC:(h + 1) * TC].astype(BF16)

    def out_send(j):
        p = role(j)

        @pl.when(p == 0)
        def _():
            za(j, 1).start()

        @pl.when(p == 3)
        def _():
            za(j, -1).start()

    def out_a(j):
        @pl.when(role(j) == 2)
        def _():
            za(j, 1).wait_recv()
            at = rows(j)
            sbuf[j // 2, at] = (ssum[j // 2, at] + ra[j // 2, at].astype(F32)).astype(BF16)
            zb(j).start()

    def out_b(j):
        @pl.when(role(j) == 1)
        def _():
            za(j, 1).wait_recv()
            zb(j).wait_recv()
            at = rows(j)
            total = ssum[j // 2, at] + ra[j // 2, at].astype(F32) + rb[j // 2, at].astype(F32)
            piece(j)[...] = total.astype(BF16)
            zc(j, 1, 1).start()
            if j in STRAIGHT:
                zc(j, 2, 2).start()
            zc(j, -1, 0).start()
            co(j).start()

    def out_c(j):
        @pl.when(role(j) == 2)
        def _():
            zc(j, 1, 0).wait_recv()
            if j not in STRAIGHT:
                zc(j, 1, 0).start()
            co(j).start()

    def out_d(j):
        p = role(j)

        @pl.when((p == 0) | (p == 3))
        def _():
            zc(j, 1, 0).wait_recv()
            co(j).start()

    def out_end(j):
        co(j).wait_recv()
        co(j).wait_send()
        p = role(j)

        @pl.when(p == 0)
        def _():
            za(j, 1).wait_send()

        @pl.when(p == 3)
        def _():
            za(j, -1).wait_send()

        @pl.when(p == 2)
        def _():
            zb(j).wait_send()
            if j not in STRAIGHT:
                zc(j, 1, 0).wait_send()

        @pl.when(p == 1)
        def _():
            zc(j, -1, 0).wait_send()
            zc(j, 1, 1).wait_send()
            if j in STRAIGHT:
                zc(j, 2, 2).wait_send()

    blocks = ((0, pv, lambda d: uv(0, d), xp, bp, fp, sp, rp), (1, pu, lambda d: uv(d, 0), xq, bq, fq, sq, rq))
    b_copies = {}

    def in_turn(st):
        for g in range(2):
            hand[st, g].wait_recv()
        for g, pos, dev, xb, bb, f, s, r in blocks:
            turned[st, g] = xb[:, :, st * TS:(st + 1) * TS].reshape(4 * KI, TS).T

    def in_partial(st):
        for g, pos, dev, xb, bb, f, s, r in blocks:
            part = jnp.dot(turned[st, g], bb[...].reshape(4 * KI, bb.shape[-1]), preferred_element_type=F32)
            f[st] = part
            s[st] = part.astype(RS)
            for i, d in enumerate(PEERS):
                to = pl.ds(pl.multiple_of(((pos + d) % 4) * TO, TO), TO)
                c = remote(s.at[st, to], r.at[st, i], b_s.at[st, g, i], b_r.at[st, g, i], dev(d))
                c.start()
                b_copies[st, g, i] = c
                sends.append(c)

    h_copies = {}

    def in_cross(st):
        for g, pos, dev, xb, bb, f, s, r in blocks:
            for i in range(3):
                b_copies[st, g, i].wait_recv()
            total = f[st, pl.ds(pl.multiple_of(pos * TO, TO), TO), :]
            for i in range(3):
                total = total + r[st, i].astype(F32)
            lanes = slice(0, WP) if g == 0 else slice(WP, DI)
            gz[st, :, lanes] = total
            zs[st, :, lanes] = total.astype(BF16)
        c = remote(zs.at[st], zr.at[st], h_s.at[st], h_r.at[st], partner)
        c.start()
        h_copies[st] = c
        sends.append(c)

    gather = (
        (0, irp, pu, pv, lambda d: uv(d, 0), lambda d: uv(0, d)),
        (1, irq, pv, pu, lambda d: uv(0, d), lambda d: uv(d, 0)),
    )
    def sub(buf, first, second, st):
        return buf.at[pl.ds(pl.multiple_of(first * 512 + st * TS + second * TO, TO), TO)]

    c1 = {}

    def in_round(st):
        h_copies[st].wait_recv()
        for g, buf, first, second, along, across in gather:
            lanes = slice(0, WP) if g == 0 else slice(WP, DI)
            whole = gz[st, :, lanes] + zr[st, :, lanes].astype(F32)
            sub(buf, first, second, st)[...] = whole.astype(BF16)
        for g, buf, first, second, along, across in gather:
            at = sub(buf, first, second, st)
            for i, d in enumerate(PEERS):
                c = remote(at, at, c1_s.at[st, g, i], c1_r.at[st, g, i], across(d))
                c.start()
                c1[st, g, i] = c
                sends.append(c)

    c2 = {}
    c3 = {}

    def slab(buf, first, st, lo, n):
        return buf.at[pl.ds(pl.multiple_of(first * 512 + st * TS + lo, 16), n)]

    def in_spread(st):
        for g, buf, first, second, along, across in gather:
            for i in range(3):
                c1[st, g, i].wait_recv()
            at = slab(buf, first, st, 0, TS)
            for side, d in enumerate(PEERS if st == NS - 1 else PEERS[:2]):
                c = remote(at, at, c2_s.at[st, g, side], c2_r.at[st, g, side], along(d))
                c.start()
                c2[st, g, side] = c
                sends.append(c)

    def in_forward(st):
        for side in range(2) if st < NS - 1 else ():
            for g, buf, first, second, along, across in gather:
                c2[st, g, side].wait_recv()
                at = slab(buf, (first + 3 - 2 * side) % 4, st, side * (TS // 2), TS // 2)
                c = remote(at, at, c3_s.at[st, g, side], c3_r.at[st, g, side], along(1 + 2 * side))
                c.start()
                c3[st, g, side] = c
                sends.append(c)

    def in_end(st):
        for g in range(2):
            if st < NS - 1:
                for side in range(2):
                    c3[st, g, side].wait_recv()
            else:
                for side in range(3):
                    c2[st, g, side].wait_recv()

    ld_ob.start()
    load_gradients(theirs, 0, 0)
    pl.semaphore_wait(barrier, 11 - ends)
    x_send(0)
    basis_send()
    load_gradients(theirs, 1, 0)
    load_gradients(mine, 0, 1)
    load_own()
    for jj, k in ((2, 0), (1, 1), (3, 0), (2, 1), (3, 1)):
        load_gradients(mine if k else theirs, jj, k)
    ld_ob.wait()
    out_theirs(0)
    x_send(1)
    out_theirs(1)
    x_send(2)
    out_mine(0)
    out_send(0)
    out_send(1)
    for c in own_loads:
        c.wait()
    x_hand(0)
    out_send(2)
    out_send(3)
    out_theirs(2)
    out_mine(1)
    in_turn(0)
    out_a(0)
    out_send(4)
    x_send(3)
    for c in b_blocks:
        c.wait_recv()
    in_partial(0)
    out_send(5)
    out_send(6)
    out_a(1)
    x_hand(1)
    out_mine(2)
    out_a(2)
    out_a(3)
    out_b(0)
    x_hand(2)
    out_send(7)
    in_turn(1)
    out_send(8)
    out_a(4)
    in_partial(1)
    x_hand(3)
    out_b(1)
    in_cross(0)
    out_send(9)
    out_a(5)
    in_turn(2)
    in_partial(2)
    out_a(6)
    out_b(2)
    out_b(3)
    in_turn(3)
    in_partial(3)
    in_cross(1)
    out_c(0)
    out_b(4)
    out_a(7)
    in_cross(2)
    out_send(10)
    out_a(8)
    out_send(11)
    out_theirs(3)
    out_c(1)
    in_cross(3)
    out_mine(3)
    out_b(5)
    out_d(0)
    out_send(12)
    in_round(0)
    out_b(6)
    out_send(13)
    out_c(2)
    out_a(9)
    out_a(10)
    out_send(14)
    in_round(1)
    out_c(3)
    out_b(7)
    out_c(4)
    out_d(1)
    in_spread(0)
    out_d(2)
    out_a(11)
    out_send(15)
    out_a(12)
    out_b(8)
    in_round(2)
    out_b(9)
    out_a(13)
    in_round(3)
    out_c(5)
    out_b(10)
    out_c(6)
    in_spread(1)
    out_a(14)
    out_d(3)
    out_b(11)
    out_c(7)
    out_a(15)
    out_b(12)
    in_forward(0)
    out_d(4)
    out_b(13)
    in_spread(2)
    out_c(8)
    out_c(9)
    out_d(5)
    out_d(6)
    in_spread(3)
    out_b(14)
    out_c(10)
    out_c(11)
    out_d(7)
    out_b(15)
    in_forward(1)
    out_d(8)
    in_forward(2)
    out_d(9)
    out_c(12)
    out_d(10)
    out_d(11)
    out_c(13)
    out_d(12)
    out_d(13)
    out_d(14)
    out_d(15)
    out_c(14)
    out_c(15)
    in_forward(3)
    for j in range(NC):
        out_end(j)
    for st in range(NS):
        in_end(st)

    for c in sends:
        c.wait_send()


def correct(orot, irp, irq, out_hbm, held, sem):
    stores = []
    for m in range(3):
        part = slice(m * 144, (m + 1) * 144)
        for lanes, ir in ((slice(0, WP), irp), (slice(WP, DI), irq)):
            acc = None
            for n in range(2):
                seq = slice(n * SEQ, (n + 1) * SEQ)
                prod = jnp.dot(orot[part, seq], ir[seq, :], preferred_element_type=F32)
                acc = prod * prod if acc is None else acc + prod * prod
            held[part, lanes] = acc * F32(1.0 / ROWS)
        c = pltpu.make_async_copy(held.at[part], out_hbm.at[part], sem.at[m])
        c.start()
        stores.append(c)
    for c in stores:
        c.wait()


def on_device(out_grads, inputs, out_basis, in_basis):
    dma = pltpu.SemaphoreType.DMA
    vm = pltpu.VMEM
    result = pl.pallas_call(
        kernel,
        out_shape=(vm((DO, ROWS), BF16), vm((ROWS, WP), BF16), vm((ROWS, WQ), BF16)),
        in_specs=[pl.BlockSpec(memory_space=pl.ANY)] * 4,
        out_specs=[pl.BlockSpec(memory_space=pltpu.VMEM)] * 3,
        scratch_shapes=[
            vm((2, 4, KO, 256), BF16), vm((DO, KO), BF16),
            vm((4, DO, 256), F32), vm((4, DO, 256), F32), vm((NC // 2, DO, TC), F32), vm((NC // 2, DO, TC), BF16),
            vm((NC // 2, DO, TC), BF16), vm((NC // 2, DO, TC), BF16),
            vm((2, 4 * HK, 512), BF16), vm((2, 4 * HK, 512), BF16), vm((NS, 2, TS, 4 * KI), BF16),
            vm((2, 4 * HK, WP), BF16), vm((2, 4 * HK, WQ), BF16),
            vm((NS, TS, WP), F32), vm((NS, TS, WQ), F32), vm((NS, TS, WP), RS), vm((NS, TS, WQ), RS),
            vm((NS, 3, TO, WP), RS), vm((NS, 3, TO, WQ), RS),
            vm((NS, TO, DI), F32), vm((NS, TO, DI), BF16), vm((NS, TO, DI), BF16),
            dma((8,)), dma((4, 2)), dma((4,)), dma((4,)), dma((NC,)), dma((NC,)),
            dma((NC,)), dma((NC,)), dma((NC,)), dma((NC,)), dma((NC, 3)), dma((NC,)),
            dma((2, 3, 2)), dma((2, 3, 2)), dma((NS, 2, 3)), dma((NS, 2, 3)), dma((NS, 2)), dma((NS, 2)),
            dma((NS, 2, 3)), dma((NS, 2, 3)), dma((NS,)), dma((NS,)),
            dma((NS, 2, 3)), dma((NS, 2, 3)), dma((NS, 2, 3)), dma((NS, 2, 3)), dma((NS, 2, 2)), dma((NS, 2, 2)),
        ],
        compiler_params=pltpu.CompilerParams(
            collective_id=0, has_side_effects=True, vmem_limit_bytes=56 * 1024 * 1024
        ),
        cost_estimate=pl.CostEstimate(flops=4_600_000_000, bytes_accessed=10_600_000, transcendentals=0),
        name="correction",
    )(out_grads.T, inputs.T, out_basis.T, in_basis)
    return pl.pallas_call(
        correct,
        out_shape=jax.ShapeDtypeStruct((DO, DI), F32),
        in_specs=[pl.BlockSpec(memory_space=pltpu.VMEM)] * 3,
        out_specs=pl.BlockSpec(memory_space=pl.ANY),
        scratch_shapes=[vm((DO, DI), F32), dma((3,))],
        compiler_params=pltpu.CompilerParams(vmem_limit_bytes=48 * 1024 * 1024),
        name="correct",
    )(*(pltpu.with_memory_space_constraint(r, pltpu.VMEM) for r in result))


def solution(mesh):
    in_specs = (P(None, "col"), P(None, "row"), P("col", "row"), P("row", "col"))
    return jax.shard_map(
        on_device, mesh=mesh, in_specs=in_specs, out_specs=P("row", "col"), check_vma=False
    )
```
